256 devices in a mesh: dp: 16 (over z_hi, y), space: 16 (over z_lo, x, core).
Axes of the slice: x: 4, y: 4, z: 8 (z_hi: 4, z_lo: 2; z = z_hi * 2 + z_lo), core: 2. Of those that a mesh axis runs over, the one named last changes fastest.
Arguments:
- queries_raw: bfloat16 [16, 6144, 2560], P('dp', 'space'), as said below
- keys_raw: bfloat16 [16, 6144, 2560], P('dp', 'space'), as said below
- values: bfloat16 [16, 6144, 2560], P('dp', 'space'), may hold values from -6 to 6
- out_grad: bfloat16 [16, 6144, 2560], P('dp', 'space'), may hold values from -288 to 288
- q_gain: float32 [2560], replicated, may hold values from 0.1 to 1.9
- k_gain: float32 [2560], replicated, may hold values from 0.1 to 1.9
Outputs:
- key_grad: bfloat16 [16, 6144, 2560], P('dp', 'space')
- value_grad: bfloat16 [16, 6144, 2560], P('dp', 'space')
- q_gain_grad: float32 [2560], replicated
- k_gain_grad: float32 [2560], replicated
The draws below stay inside these ranges and needn't reach their ends.
Inputs may be any that keep to these rules, and one draw needn't show every extreme that they name: `queries_raw`: Real-valued projections. `keys_raw`: Real-valued projections.
All inputs are finite; a program needn't handle non-finite values.
Results may differ from the reference program's by a relative error of at most 0.012.
The reference program's roundings to bfloat16 on the way (of `query`, `key`, `probs_b` and `dscores`) count: a program that leaves them out, or rounds other values in their place, can miss the bound.
Values may be sent and summed in bfloat16 or wider, within the bound.
A program may use at most 128 MiB of HBM per device.

```python
import math
import jax
import jax.numpy as jnp
from jax import lax

HEADS = 20
HS = 128
R = 192
HD = 2560
TILES = 32
TOKENS = 6144
CLIPS = 16


def scaled_field(key, noise):
    row_scale = jnp.exp(jax.random.uniform(jax.random.fold_in(key, 21), (CLIPS, TOKENS, 1), jnp.float32) * math.log(10.0))
    col_scale = jnp.exp(jax.random.uniform(jax.random.fold_in(key, 22), (HEADS * HS,), jnp.float32) * math.log(10.0))
    return noise * row_scale * col_scale


def draw_queries_raw(key, part):
    key = jax.random.fold_in(key, 3)
    shape = (CLIPS, TOKENS, HEADS * HS)
    noise = jnp.clip(jax.random.normal(key, shape, jnp.float32), -4.0, 4.0)
    field = scaled_field(key, noise)
    return field.astype(jnp.bfloat16)


def draw_keys_raw(key, part):
    key = jax.random.fold_in(key, 4)
    shape = (CLIPS, TOKENS, HEADS * HS)
    noise = jnp.clip(jax.random.normal(key, shape, jnp.float32), -4.0, 4.0)
    field = scaled_field(key, noise)
    return field.astype(jnp.bfloat16)


def block_scale(stream_key, shape, cuts, least, top_value):
    def one(axis_at, parts):
        heights = jax.random.uniform(jax.random.fold_in(jax.random.fold_in(stream_key, 6), axis_at), (parts,), jnp.float32, least / len(cuts), top_value / len(cuts))
        return jnp.repeat(jnp.exp(heights), shape[axis_at] // parts).reshape((-1,) + (1,) * (len(shape) - axis_at - 1))

    factor_of = one(*cuts[0])
    for cut in cuts[1:]:
        factor_of = factor_of * one(*cut)
    return factor_of


def bell_draw(key, dims, scale, most, split=(), kind=jnp.bfloat16):
    entries = scale * jax.random.normal(key, dims, jnp.float32)
    if split:
        entries = entries * block_scale(key, dims, split, -0.22, 0.18)
    return jnp.clip(entries, -most, most).astype(kind)


def setup_inputs(seed: int = 0) -> dict:
    seeds = jax.random.split(jax.random.key(seed), 7)
    queries_raw = draw_queries_raw(jax.random.fold_in(seeds[6], 71), 0)
    keys_raw = draw_keys_raw(jax.random.fold_in(seeds[6], 71), 0)
    values = bell_draw(seeds[2], (CLIPS, TOKENS, HD), 1.0, 6.0, ((0, 16), (1, 16)))
    out_grad = bell_draw(seeds[3], (CLIPS, TOKENS, HD), 48.0, 288.0, ((0, 16), (1, 16)))
    q_gain = jnp.clip(1.0 + 0.18 * jax.random.normal(seeds[4], (HD,), jnp.float32), 0.1, 1.9)
    k_gain = jnp.clip(1.0 + 0.18 * jax.random.normal(seeds[5], (HD,), jnp.float32), 0.1, 1.9)
    return {"queries_raw": queries_raw, "keys_raw": keys_raw, "values": values, "out_grad": out_grad, "q_gain": q_gain, "k_gain": k_gain}


epsilon = 1e-06

def normalize(raw):
    wide = raw.astype(jnp.float32)
    inverse = lax.rsqrt(lax.optimization_barrier(jnp.mean(wide * wide, axis=-1, keepdims=True)) + epsilon)
    return (wide * inverse, inverse)

def rounded(array):
    narrow = lax.optimization_barrier(array.astype(jnp.bfloat16))
    return narrow.astype(jnp.float32)

def tile_grads(query, keys, values, grad_out):
    scale = HS ** (-0.5)
    query32 = query.astype(jnp.float32)
    keys32 = keys.astype(jnp.float32)
    values32 = values.astype(jnp.float32)
    grad32 = grad_out.astype(jnp.float32)
    scores = jnp.einsum('qhd,khd->hqk', query32, keys32) * scale
    top = lax.optimization_barrier(jnp.max(scores, axis=-1, keepdims=True))
    expo = jnp.exp(scores - top)
    total = lax.optimization_barrier(jnp.sum(expo, axis=-1, keepdims=True))
    probs = expo / total
    probs_b = rounded(probs)
    attn = jnp.einsum('hqk,khd->qhd', probs_b, values32)
    delta = lax.optimization_barrier(jnp.sum(grad32 * attn, axis=-1)).T
    dprobs = jnp.einsum('qhd,khd->hqk', grad32, values32)
    dscores = rounded(probs * (dprobs - delta[:, :, None]))
    dquery = jnp.einsum('hqk,khd->qhd', dscores, keys32) * scale
    dkey = jnp.einsum('hqk,qhd->khd', dscores, query32) * scale
    dvalue = jnp.einsum('hqk,qhd->khd', probs_b, grad32)
    return (dquery, dkey, dvalue)

def reference(queries_raw, keys_raw, values, out_grad, q_gain, k_gain):
    pairs = TILES // 2

    def one_clip(inputs):
        q_raw, k_raw, value, grad_out = inputs
        qn, q_inverse = normalize(q_raw)
        kn, k_inverse = normalize(k_raw)
        query = (qn * q_gain).astype(jnp.bfloat16)
        key = (kn * k_gain).astype(jnp.bfloat16)
        query_tiles = query.reshape(TILES, R, HEADS, HS)
        grad_tiles = grad_out.reshape(TILES, R, HEADS, HS)
        empty_tile = jnp.zeros((1, R, HEADS, HS), jnp.bfloat16)
        padded_keys = jnp.concatenate([empty_tile, key.reshape(TILES, R, HEADS, HS), empty_tile], axis=0)
        padded_values = jnp.concatenate([empty_tile, value.reshape(TILES, R, HEADS, HS), empty_tile], axis=0)

        def per_pair(pair):
            near_keys = lax.dynamic_slice_in_dim(padded_keys, 2 * pair, 4, 0)
            near_values = lax.dynamic_slice_in_dim(padded_values, 2 * pair, 4, 0)
            key_terms = jnp.zeros((4, R, HD), jnp.float32)
            value_terms = jnp.zeros((4, R, HD), jnp.float32)
            query_grads = []
            for which_tile in range(2):
                tile = 2 * pair + which_tile
                offset = (jnp.clip(tile, 1, TILES - 2) - 2 * pair).astype(jnp.int32)
                window_keys = lax.dynamic_slice_in_dim(near_keys, offset, 3, 0).reshape(3 * R, HEADS, HS)
                window_values = lax.dynamic_slice_in_dim(near_values, offset, 3, 0).reshape(3 * R, HEADS, HS)
                own_query = lax.dynamic_index_in_dim(query_tiles, tile, 0, keepdims=False)
                own_grad = lax.dynamic_index_in_dim(grad_tiles, tile, 0, keepdims=False)
                dquery, dkey, dvalue = tile_grads(own_query, window_keys, window_values, own_grad)
                key_terms = lax.dynamic_update_slice_in_dim(key_terms, lax.dynamic_slice_in_dim(key_terms, offset, 3, 0) + dkey.reshape(3, R, HD), offset, 0)
                value_terms = lax.dynamic_update_slice_in_dim(value_terms, lax.dynamic_slice_in_dim(value_terms, offset, 3, 0) + dvalue.reshape(3, R, HD), offset, 0)
                query_grads.append(dquery.reshape(R, HD))
            return (jnp.stack(query_grads), key_terms, value_terms)
        dquery, key_terms, value_terms = lax.map(per_pair, jnp.arange(pairs, dtype=jnp.int32))
        empty_rows = jnp.zeros((1, R, HD), jnp.float32)

        def combine(terms):
            from_left = jnp.concatenate([empty_rows, rounded(terms[:-1, 3])], axis=0)
            from_right = jnp.concatenate([rounded(terms[1:, 0]), empty_rows], axis=0)
            return (terms[:, 1:3] + jnp.stack([from_left, from_right], axis=1)).reshape(TOKENS, HD)
        key_total = combine(key_terms)
        value_total = combine(value_terms)
        dkn = key_total * k_gain
        key_grad = (k_inverse * (dkn - kn * lax.optimization_barrier(jnp.mean(dkn * kn, axis=-1, keepdims=True)))).astype(jnp.bfloat16)
        value_grad = value_total.astype(jnp.bfloat16)
        q_part = lax.optimization_barrier(jnp.sum(dquery.reshape(TOKENS, HD) * qn, axis=0))
        k_part = lax.optimization_barrier(jnp.sum(key_total * kn, axis=0))
        return (key_grad, value_grad, q_part, k_part)
    key_grad, value_grad, q_parts, k_parts = lax.map(one_clip, (queries_raw, keys_raw, values, out_grad))
    factor = (CLIPS * TOKENS) ** (-0.5)
    q_gain_grad = lax.optimization_barrier(jnp.sum(q_parts, axis=0)) * factor
    k_gain_grad = lax.optimization_barrier(jnp.sum(k_parts, axis=0)) * factor
    return (key_grad, value_grad, q_gain_grad, k_gain_grad)
```

```python
import functools
import math

import jax
import jax.numpy as jnp
from jax import lax
from jax.experimental import pallas as pl
from jax.experimental.pallas import tpu as pltpu
from jax.sharding import PartitionSpec as P

HS = 128
EPS = 1e-06
SCALE = HS ** (-0.5)
LOG_SCALE = SCALE * math.log2(math.e)
LAG = 4
CHUNK = 32
MESH = pl.DeviceIdType.MESH
NT = (((1,), (1,)), ((), ()))
NN = (((1,), (0,)), ((), ()))


def dot(a, b, dims):
    return lax.dot_general(a, b, dims, preferred_element_type=jnp.float32)


def sum_stages(dp, space):
    def pairs(axis, bits):
        return [(axis, tuple(bits[i : i + 2])) for i in range(0, len(bits), 2)]

    space_bits = list(range(space.bit_length() - 1))
    if len(space_bits) == 4:
        space_bits = [0, 3, 1, 2]
    return pairs("space", space_bits) + pairs("dp", list(range(dp.bit_length() - 1)))


def group_place(index, bits):
    digits = [(index // 2**bit) % 2 for bit in bits]
    place = sum(digit * 2**at for at, digit in enumerate(digits))
    base = index - sum(digit * 2**bit for digit, bit in zip(digits, bits))

    def member(other):
        return base + sum(((other // 2**at) % 2) * 2**bit for at, bit in enumerate(bits))

    return place, member


def kernel(
    stages,
    space,
    factor,
    q_hbm,
    k_hbm,
    v_hbm,
    g_hbm,
    q_gain,
    k_gain,
    k_out,
    v_out,
    q_gain_out,
    k_gain_out,
    q_raw,
    k_raw,
    value,
    own,
    key,
    k_inv,
    near,
    extra,
    e_own,
    p_own,
    e_near,
    p_near,
    e_extra,
    p_extra,
    dk,
    dv,
    v_grad,
    row_dot,
    own_stat,
    near_stat,
    extra_stat,
    to_left,
    to_right,
    from_left,
    from_right,
    gain_part,
    gain_box,
    load_sem,
    g_sem,
    near_send,
    near_recv,
    extra_send,
    extra_recv,
    stat_send,
    stat_recv,
    v_sem,
    k_sem,
    gain_send,
    gain_recv,
):
    me = lax.axis_index("space")
    heads, _, rows, _ = own.shape
    tile = rows // 2
    features = heads * HS
    low, high = pl.ds(0, tile), pl.ds(tile, tile)
    first, second = pl.ds(0, HS), pl.ds(HS, HS)
    has_left, has_right = me > 0, me < space - 1
    extra_left, extra_right = me == 1, me == space - 2
    is_extra = jnp.logical_or(extra_left, extra_right)
    left, right = {"space": me - 1}, {"space": me + 1}

    def columns(head):
        return pl.ds(pl.multiple_of(head * HS, HS), HS)

    load_q = pltpu.make_async_copy(q_hbm, q_raw, load_sem.at[0])
    load_k = pltpu.make_async_copy(k_hbm, k_raw, load_sem.at[1])
    load_v = pltpu.make_async_copy(v_hbm, value, load_sem.at[2])

    def load_g(head):
        return pltpu.make_async_copy(g_hbm.at[:, columns(head)], own.at[head, 1], g_sem.at[head])

    load_q.start()

    @pl.loop(0, heads)
    def _(head):
        load_g(head).start()

    load_k.start()
    load_v.start()

    barrier = pltpu.get_barrier_semaphore()

    @pl.when(has_left)
    def _():
        pl.semaphore_signal(barrier, inc=1, device_id=left, device_id_type=MESH)

    @pl.when(has_right)
    def _():
        pl.semaphore_signal(barrier, inc=1, device_id=right, device_id_type=MESH)

    partners = 0
    for axis, bits in stages:
        place, member = group_place(lax.axis_index(axis), bits)
        size = 2 ** len(bits)
        for step in range(1, size):
            pl.semaphore_signal(
                barrier,
                inc=1,
                device_id={axis: member((place + step) % size)},
                device_id_type=MESH,
            )
            partners += 1

    zeros = jnp.zeros((2, tile, HS), jnp.bfloat16)

    @pl.loop(0, heads)
    def _(head):
        near[head, :, low, first] = zeros
        near[head, :, high, second] = zeros

        @pl.when(jnp.logical_not(has_left))
        def _():
            near[head, :, high, first] = zeros
            from_left[head] = jnp.zeros(from_left.shape[1:], jnp.float32)

        @pl.when(jnp.logical_not(has_right))
        def _():
            near[head, :, low, second] = zeros
            from_right[head] = jnp.zeros(from_right.shape[1:], jnp.float32)

        @pl.when(is_extra)
        def _():
            extra[head, :, low, second] = zeros
            extra[head, :, high, first] = zeros

        @pl.when(jnp.logical_and(is_extra, jnp.logical_not(extra_left)))
        def _():
            extra[head, :, low, first] = zeros

        @pl.when(jnp.logical_and(is_extra, jnp.logical_not(extra_right)))
        def _():
            extra[head, :, high, second] = zeros

    extra_stat[...] = jnp.zeros_like(extra_stat)
    row_dot[...] = jnp.zeros_like(row_dot)
    gain_part[...] = jnp.zeros_like(gain_part)

    load_q.wait()

    def normalize(raw, gain, row_begin, put):
        span = pl.ds(pl.multiple_of(row_begin, CHUNK), CHUNK)
        total = jnp.zeros((CHUNK, HS), jnp.float32)
        for head in range(heads):
            wide = raw[span, head * HS : (head + 1) * HS].astype(jnp.float32)
            total = total + wide * wide
        mean = jnp.sum(total, axis=-1, keepdims=True) * (1.0 / features)
        inverse = lax.rsqrt(mean + EPS)
        for head in range(heads):
            wide = raw[span, head * HS : (head + 1) * HS].astype(jnp.float32)
            put(
                head,
                span,
                (wide * inverse * gain[:, head * HS : (head + 1) * HS]).astype(jnp.bfloat16),
            )
        return span, inverse

    def put_query(head, span, block):
        own[head, 0, span, :] = block

    def put_key(head, span, block):
        key[head, span, :] = block

    @pl.loop(0, rows // CHUNK)
    def _(chunk):
        normalize(q_raw, q_gain, chunk * CHUNK, put_query)

    count = partners + has_left.astype(jnp.int32) + has_right.astype(jnp.int32)
    pl.semaphore_wait(barrier, count)

    def near_to_right(head):
        return pltpu.make_async_remote_copy(
            src_ref=own.at[head, :, high, :],
            dst_ref=near.at[head, :, high, first],
            send_sem=near_send.at[0, head],
            recv_sem=near_recv.at[0, head],
            device_id=right,
            device_id_type=MESH,
        )

    def near_to_left(head):
        return pltpu.make_async_remote_copy(
            src_ref=own.at[head, :, low, :],
            dst_ref=near.at[head, :, low, second],
            send_sem=near_send.at[1, head],
            recv_sem=near_recv.at[1, head],
            device_id=left,
            device_id_type=MESH,
        )

    def extra_to_right(head):
        return pltpu.make_async_remote_copy(
            src_ref=own.at[head, :, low, :],
            dst_ref=extra.at[head, :, low, first],
            send_sem=extra_send.at[0, head],
            recv_sem=extra_recv.at[0, head],
            device_id=right,
            device_id_type=MESH,
        )

    def extra_to_left(head):
        return pltpu.make_async_remote_copy(
            src_ref=own.at[head, :, high, :],
            dst_ref=extra.at[head, :, high, second],
            send_sem=extra_send.at[1, head],
            recv_sem=extra_recv.at[1, head],
            device_id=left,
            device_id_type=MESH,
        )

    @pl.loop(0, heads)
    def _(head):
        load_g(head).wait()

        @pl.when(has_right)
        def _():
            near_to_right(head).start()

        @pl.when(has_left)
        def _():
            near_to_left(head).start()

        @pl.when(jnp.logical_not(has_left))
        def _():
            extra_to_right(head).start()

        @pl.when(jnp.logical_not(has_right))
        def _():
            extra_to_left(head).start()

    load_k.wait()

    @pl.loop(0, rows // CHUNK)
    def _(chunk):
        span, inverse = normalize(k_raw, k_gain, chunk * CHUNK, put_key)
        k_inv[span, :] = jnp.broadcast_to(inverse, (CHUNK, HS))

    load_v.wait()

    in_low = lax.broadcasted_iota(jnp.int32, (1, rows), 1) < tile

    def stat_to_left(head):
        return pltpu.make_async_remote_copy(
            src_ref=to_left.at[head],
            dst_ref=from_right.at[head],
            send_sem=stat_send.at[0, head],
            recv_sem=stat_recv.at[0, head],
            device_id=left,
            device_id_type=MESH,
        )

    def stat_to_right(head):
        return pltpu.make_async_remote_copy(
            src_ref=to_right.at[head],
            dst_ref=from_left.at[head],
            send_sem=stat_send.at[1, head],
            recv_sem=stat_recv.at[1, head],
            device_id=right,
            device_id_type=MESH,
        )

    def wide_pair(block):
        return jnp.concatenate([block[:tile], block[tile:]], axis=1)

    def scores(keys, values, queries, grads, e_ref, p_ref):
        score = dot(keys, queries, NT)
        top = jnp.max(score, axis=0, keepdims=True)
        expo = jnp.exp2((score - top) * LOG_SCALE)
        dprobs = dot(values, grads, NT)
        e_ref[...] = expo
        p_ref[...] = dprobs
        return (
            top,
            jnp.sum(expo, axis=0, keepdims=True),
            jnp.sum(expo * dprobs, axis=0, keepdims=True),
        )

    def put_stat(ref, slot, stat):
        for at, row in enumerate(stat):
            ref[slot, at : at + 1, :] = row

    def forward(head):
        slot = head % (LAG + 1)
        keys, values = key[head], value[:, columns(head)]
        stat = scores(keys, values, own[head, 0], own[head, 1], e_own.at[slot], p_own.at[slot])
        put_stat(own_stat, head, stat)
        stat = scores(
            wide_pair(keys),
            wide_pair(values),
            near[head, 0],
            near[head, 1],
            e_near.at[slot],
            p_near.at[slot],
        )
        put_stat(near_stat, head, stat)

    def forward_extra(head):
        slot = head % (LAG + 1)
        stat = scores(
            wide_pair(key[head]),
            wide_pair(value[:, columns(head)]),
            extra[head, 0],
            extra[head, 1],
            e_extra.at[slot],
            p_extra.at[slot],
        )
        put_stat(extra_stat, head, stat)

    def tell(head):
        near_now, extra_now = near_stat[head], extra_stat[head]
        to_left[head, 0:8, :] = own_stat[head]
        to_left[head, 8:16, :] = jnp.where(in_low, extra_now, near_now)
        to_right[head, 0:8, :] = own_stat[head]
        to_right[head, 8:16, :] = jnp.where(in_low, near_now, extra_now)

        @pl.when(has_left)
        def _():
            stat_to_left(head).start()

        @pl.when(has_right)
        def _():
            stat_to_right(head).start()

    def merge(mine, other):
        top = jnp.maximum(mine[0:1], other[0:1])
        a = jnp.exp2((mine[0:1] - top) * LOG_SCALE)
        b = jnp.exp2((other[0:1] - top) * LOG_SCALE)
        inverse = 1.0 / (mine[1:2] * a + other[1:2] * b)
        return a * inverse, (mine[2:3] * a + other[2:3] * b) * inverse

    def backward_terms(e_ref, p_ref, mine, other, queries, grads):
        weight, delta = merge(mine, other)
        probs = e_ref[...] * weight
        dscores = (probs * (p_ref[...] - delta)).astype(jnp.bfloat16)
        return dot(dscores, queries, NN), dot(probs.astype(jnp.bfloat16), grads, NN)

    def backward(head):
        slot = head % (LAG + 1)
        left_stat, right_stat = from_left[head], from_right[head]
        from_low = jnp.logical_and(jnp.logical_or(in_low, me == space - 1), me > 0)
        other = jnp.where(from_low, left_stat[8:16], right_stat[8:16])
        dkey, dvalue = backward_terms(
            e_own.at[slot], p_own.at[slot], own_stat[head], other, own[head, 0], own[head, 1]
        )
        other = jnp.where(in_low, right_stat[0:8], left_stat[0:8])
        near_dkey, near_dvalue = backward_terms(
            e_near.at[slot], p_near.at[slot], near_stat[head], other, near[head, 0], near[head, 1]
        )
        dk[head, low, :] = dkey[:tile] + near_dkey[:, :HS]
        dk[head, high, :] = dkey[tile:] + near_dkey[:, HS:]
        dv[low, :] = dvalue[:tile] + near_dvalue[:, :HS]
        dv[high, :] = dvalue[tile:] + near_dvalue[:, HS:]

    def backward_extra(head):
        slot = head % (LAG + 1)
        other = jnp.where(in_low, from_left[head, 0:8, :], from_right[head, 0:8, :])
        dkey, dvalue = backward_terms(
            e_extra.at[slot],
            p_extra.at[slot],
            extra_stat[head],
            other,
            extra[head, 0],
            extra[head, 1],
        )
        dk[head, low, :] += dkey[:, :HS]
        dk[head, high, :] += dkey[:, HS:]
        dv[low, :] += dvalue[:, :HS]
        dv[high, :] += dvalue[:, HS:]

    def store_v(head):
        return pltpu.make_async_copy(v_grad.at[head], v_out.at[:, columns(head)], v_sem.at[head])

    def finish(head):
        v_grad[head] = dv[...].astype(jnp.bfloat16)
        store_v(head).start()
        total = dk[head] * SCALE
        kn = k_raw[:, columns(head)].astype(jnp.float32) * k_inv[...]
        gain_part[pl.ds(head, 1), :] = jnp.sum(total * kn, axis=0, keepdims=True)
        dkn = total * k_gain[:, columns(head)]
        dk[head] = dkn
        row_dot[...] += dkn * kn

    def wait_near(head):
        @pl.when(has_left)
        def _():
            near_to_right(head).wait_recv()

        @pl.when(has_right)
        def _():
            near_to_left(head).wait_recv()

        @pl.when(extra_left)
        def _():
            extra_to_right(head).wait_recv()

        @pl.when(extra_right)
        def _():
            extra_to_left(head).wait_recv()

    def wait_stat(head):
        @pl.when(has_left)
        def _():
            stat_to_right(head).wait_recv()

        @pl.when(has_right)
        def _():
            stat_to_left(head).wait_recv()

    @pl.loop(0, LAG)
    def _(head):
        wait_near(head)
        forward(head)

        @pl.when(is_extra)
        def _():
            forward_extra(head)

        tell(head)

    @pl.loop(LAG, heads)
    def _(head):
        behind = head - LAG
        wait_near(head)
        wait_stat(behind)
        forward(head)
        backward(behind)

        @pl.when(is_extra)
        def _():
            forward_extra(head)
            backward_extra(behind)

        tell(head)
        finish(behind)

    @pl.loop(heads - LAG, heads)
    def _(head):
        wait_stat(head)
        backward(head)

        @pl.when(is_extra)
        def _():
            backward_extra(head)

        finish(head)

    mean = jnp.sum(row_dot[...], axis=-1, keepdims=True) * (1.0 / features)
    row_dot[...] = jnp.broadcast_to(mean, row_dot.shape)

    def store_k(head):
        columns_now = slice(head * HS, (head + 1) * HS)
        return pltpu.make_async_copy(
            q_raw.at[:, columns_now], k_out.at[:, columns_now], k_sem.at[head]
        )

    def key_pass(head):
        kn = k_raw[:, head * HS : (head + 1) * HS].astype(jnp.float32) * k_inv[...]
        q_raw[:, head * HS : (head + 1) * HS] = (
            k_inv[...] * (dk[head] - kn * row_dot[...])
        ).astype(jnp.bfloat16)
        store_k(head).start()

    total = gain_part[...]
    done = 0
    for at, (axis, bits) in enumerate(stages):
        place, member = group_place(lax.axis_index(axis), bits)
        size = 2 ** len(bits)
        gain_box[at, pl.ds(place, 1)] = total[None]
        copies = [
            pltpu.make_async_remote_copy(
                src_ref=gain_box.at[at, place],
                dst_ref=gain_box.at[at, place],
                send_sem=gain_send.at[at, step],
                recv_sem=gain_recv.at[at, step],
                device_id={axis: member((place + step) % size)},
                device_id_type=MESH,
            )
            for step in range(1, size)
        ]
        for copy in copies:
            copy.start()
        until = heads * (at + 1) // len(stages)
        for head in range(done, until):
            key_pass(head)
        done = until
        for step in range(1, size):
            source = (place + size - step) % size
            pltpu.make_async_remote_copy(
                src_ref=gain_box.at[at, place],
                dst_ref=gain_box.at[at, source],
                send_sem=gain_send.at[at, step],
                recv_sem=gain_recv.at[at, step],
                device_id={axis: member((place + step) % size)},
                device_id_type=MESH,
            ).wait_recv()
        total = gain_box[at, 0]
        for other in range(1, size):
            total = total + gain_box[at, other]
        for copy in copies:
            copy.wait_send()

    result = total[:heads] * factor
    k_gain_out[...] = result
    q_gain_out[...] = result
    for head in range(heads):
        cut = slice(head * HS, (head + 1) * HS)
        q_gain_out[head : head + 1, :] = (
            result[head : head + 1] * k_gain[:, cut] / q_gain[:, cut]
        )

    @pl.loop(0, heads)
    def _(head):
        store_v(head).wait()

        @pl.when(has_right)
        def _():
            near_to_right(head).wait_send()
            stat_to_right(head).wait_send()

        @pl.when(has_left)
        def _():
            near_to_left(head).wait_send()
            stat_to_left(head).wait_send()

        @pl.when(jnp.logical_not(has_left))
        def _():
            extra_to_right(head).wait_send()

        @pl.when(jnp.logical_not(has_right))
        def _():
            extra_to_left(head).wait_send()

    for head in range(heads):
        store_k(head).wait()


def per_device(queries_raw, keys_raw, values, out_grad, q_gain, k_gain):
    _, rows, features = queries_raw.shape
    heads = features // HS
    tile = rows // 2
    dp, space = lax.axis_size("dp"), lax.axis_size("space")
    stages = sum_stages(dp, space)
    factor = (dp * space * rows) ** (-0.5)
    slots = LAG + 1
    bf16, f32 = jnp.bfloat16, jnp.float32
    padded = (heads + 7) // 8 * 8
    hbm = pl.BlockSpec(memory_space=pl.ANY)
    vmem = pl.BlockSpec(memory_space=pltpu.VMEM)
    dma = pltpu.SemaphoreType.DMA
    key_grad, value_grad, q_sum, k_sum = pl.pallas_call(
        functools.partial(kernel, stages, space, factor),
        out_shape=(
            jax.ShapeDtypeStruct((rows, features), bf16),
            jax.ShapeDtypeStruct((rows, features), bf16),
            jax.ShapeDtypeStruct((heads, HS), f32),
            jax.ShapeDtypeStruct((heads, HS), f32),
        ),
        in_specs=[hbm] * 4 + [vmem] * 2,
        out_specs=(hbm, hbm, vmem, vmem),
        scratch_shapes=[
            pltpu.VMEM((rows, features), bf16),
            pltpu.VMEM((rows, features), bf16),
            pltpu.VMEM((rows, features), bf16),
            pltpu.VMEM((heads, 2, rows, HS), bf16),
            pltpu.VMEM((heads, rows, HS), bf16),
            pltpu.VMEM((rows, HS), f32),
            pltpu.VMEM((heads, 2, rows, 2 * HS), bf16),
            pltpu.VMEM((heads, 2, rows, 2 * HS), bf16),
            pltpu.VMEM((slots, rows, rows), f32),
            pltpu.VMEM((slots, rows, rows), f32),
            pltpu.VMEM((slots, tile, rows), f32),
            pltpu.VMEM((slots, tile, rows), f32),
            pltpu.VMEM((slots, tile, rows), f32),
            pltpu.VMEM((slots, tile, rows), f32),
            pltpu.VMEM((heads, rows, HS), f32),
            pltpu.VMEM((rows, HS), f32),
            pltpu.VMEM((heads, rows, HS), bf16),
            pltpu.VMEM((rows, HS), f32),
            pltpu.VMEM((heads, 8, rows), f32),
            pltpu.VMEM((heads, 8, rows), f32),
            pltpu.VMEM((heads, 8, rows), f32),
            pltpu.VMEM((heads, 16, rows), f32),
            pltpu.VMEM((heads, 16, rows), f32),
            pltpu.VMEM((heads, 16, rows), f32),
            pltpu.VMEM((heads, 16, rows), f32),
            pltpu.VMEM((padded, HS), f32),
            pltpu.VMEM((len(stages), 4, padded, HS), f32),
            dma((3,)),
            dma((heads,)),
            dma((2, heads)),
            dma((2, heads)),
            dma((2, heads)),
            dma((2, heads)),
            dma((2, heads)),
            dma((2, heads)),
            dma((heads,)),
            dma((heads,)),
            dma((len(stages), 4)),
            dma((len(stages), 4)),
        ],
        compiler_params=pltpu.CompilerParams(
            collective_id=0, has_side_effects=True, vmem_limit_bytes=60 * 2**20
        ),
    )(
        queries_raw[0],
        keys_raw[0],
        values[0],
        out_grad[0],
        q_gain.reshape(1, features),
        k_gain.reshape(1, features),
    )
    return key_grad[None], value_grad[None], q_sum.reshape(features), k_sum.reshape(features)


def solution(mesh):
    split = P("dp", "space", None)
    return jax.shard_map(
        per_device,
        mesh=mesh,
        in_specs=(split, split, split, split, P(), P()),
        out_specs=(split, split, P(), P()),
        check_vma=False,
    )
```

```python
import functools
import math

import jax
import jax.numpy as jnp
from jax import lax
from jax.experimental import pallas as pl
from jax.experimental.pallas import tpu as pltpu
from jax.sharding import PartitionSpec as P

HS = 128
EPS = 1e-06
SCALE = HS ** (-0.5)
LOG_SCALE = SCALE * math.log2(math.e)
LAG = 4
FINISH_LAG = 2
LEAD = 5
CHUNK = 32
MESH = pl.DeviceIdType.MESH
NT = (((1,), (1,)), ((), ()))
NN = (((1,), (0,)), ((), ()))


def dot(a, b, dims):
    return lax.dot_general(a, b, dims, preferred_element_type=jnp.float32)


def sum_stages(dp, space):
    def pairs(axis, bits):
        return [(axis, tuple(bits[i : i + 2])) for i in range(0, len(bits), 2)]

    space_bits = list(range(space.bit_length() - 1))
    if len(space_bits) == 4:
        space_bits = [0, 3, 1, 2]
    return pairs("space", space_bits) + pairs("dp", list(range(dp.bit_length() - 1)))


def group_place(index, bits):
    digits = [(index // 2**bit) % 2 for bit in bits]
    place = sum(digit * 2**at for at, digit in enumerate(digits))
    base = index - sum(digit * 2**bit for digit, bit in zip(digits, bits))

    def member(other):
        return base + sum(((other // 2**at) % 2) * 2**bit for at, bit in enumerate(bits))

    return place, member


def kernel(
    stages,
    space,
    factor,
    q_hbm,
    k_hbm,
    v_hbm,
    g_hbm,
    q_gain_flat,
    k_gain_flat,
    k_out,
    v_out,
    q_gain_out,
    k_gain_out,
    q_raw,
    k_raw,
    value,
    own,
    key,
    k_inv,
    near,
    edge_keys,
    e_own,
    p_own,
    e_near,
    p_near,
    dk,
    dv,
    v_grad,
    row_dot,
    own_stat,
    near_stat,
    to_left,
    to_right,
    from_left,
    from_right,
    edge_out,
    edge_in,
    gain_part,
    gain_box,
    q_gain,
    k_gain,
    load_sem,
    g_sem,
    near_send,
    near_recv,
    keys_send,
    keys_recv,
    edge_send,
    edge_recv,
    stat_send,
    stat_recv,
    v_sem,
    k_sem,
    gain_send,
    gain_recv,
):
    me = lax.axis_index("space")
    heads, _, rows, _ = own.shape
    tile = rows // 2
    features = heads * HS
    low, high = pl.ds(0, tile), pl.ds(tile, tile)
    first, second = pl.ds(0, HS), pl.ds(HS, HS)
    has_left, has_right = me > 0, me < space - 1
    beside_first, beside_last = me == 1, me == space - 2
    left, right = {"space": me - 1}, {"space": me + 1}

    def columns(head):
        return pl.ds(pl.multiple_of(head * HS, HS), HS)

    load_q = pltpu.make_async_copy(q_hbm, q_raw, load_sem.at[0])
    load_k = pltpu.make_async_copy(k_hbm, k_raw, load_sem.at[1])
    load_v = pltpu.make_async_copy(v_hbm, value, load_sem.at[2])

    def load_g(head):
        return pltpu.make_async_copy(g_hbm.at[:, columns(head)], own.at[head, 1], g_sem.at[head])

    load_q.start()

    @pl.loop(0, heads)
    def _(head):
        load_g(head).start()

    load_k.start()
    load_v.start()

    barrier = pltpu.get_barrier_semaphore()

    @pl.when(has_left)
    def _():
        pl.semaphore_signal(barrier, inc=1, device_id=left, device_id_type=MESH)

    @pl.when(has_right)
    def _():
        pl.semaphore_signal(barrier, inc=1, device_id=right, device_id_type=MESH)

    partners = 0
    for axis, bits in stages:
        place, member = group_place(lax.axis_index(axis), bits)
        size = 2 ** len(bits)
        for step in range(1, size):
            pl.semaphore_signal(
                barrier,
                inc=1,
                device_id={axis: member((place + step) % size)},
                device_id_type=MESH,
            )
            partners += 1

    zeros = jnp.zeros((2, tile, HS), jnp.bfloat16)

    @pl.loop(0, heads)
    def _(head):
        near[head, :, low, first] = zeros
        near[head, :, high, second] = zeros

    row_dot[...] = jnp.zeros_like(row_dot)
    gain_part[...] = jnp.zeros_like(gain_part)

    for head in range(heads):
        cut = slice(head * HS, (head + 1) * HS)
        q_gain[:, cut] = q_gain_flat[cut].reshape(1, HS)
        k_gain[:, cut] = k_gain_flat[cut].reshape(1, HS)

    load_q.wait()

    def normalize(raw, gain, row_begin, put):
        span = pl.ds(pl.multiple_of(row_begin, CHUNK), CHUNK)
        total = jnp.zeros((CHUNK, HS), jnp.float32)
        for head in range(heads):
            wide = raw[span, head * HS : (head + 1) * HS].astype(jnp.float32)
            total = total + wide * wide
        mean = jnp.sum(total, axis=-1, keepdims=True) * (1.0 / features)
        inverse = lax.rsqrt(mean + EPS)
        for head in range(heads):
            wide = raw[span, head * HS : (head + 1) * HS].astype(jnp.float32)
            put(
                head,
                span,
                (wide * inverse * gain[:, head * HS : (head + 1) * HS]).astype(jnp.bfloat16),
            )
        return span, inverse

    def put_query(head, span, block):
        own[head, 0, span, :] = block

    def put_key(head, span, block):
        key[head, span, :] = block

    @pl.loop(0, rows // CHUNK)
    def _(chunk):
        normalize(q_raw, q_gain, chunk * CHUNK, put_query)

    count = partners + has_left.astype(jnp.int32) + has_right.astype(jnp.int32)
    pl.semaphore_wait(barrier, count)

    def near_to_right(head):
        return pltpu.make_async_remote_copy(
            src_ref=own.at[head, :, high, :],
            dst_ref=near.at[head, :, high, first],
            send_sem=near_send.at[0, head],
            recv_sem=near_recv.at[0, head],
            device_id=right,
            device_id_type=MESH,
        )

    def near_to_left(head):
        return pltpu.make_async_remote_copy(
            src_ref=own.at[head, :, low, :],
            dst_ref=near.at[head, :, low, second],
            send_sem=near_send.at[1, head],
            recv_sem=near_recv.at[1, head],
            device_id=left,
            device_id_type=MESH,
        )

    def keys_to_first(head):
        return [
            pltpu.make_async_remote_copy(
                src_ref=source,
                dst_ref=edge_keys.at[head, at],
                send_sem=keys_send.at[at, head],
                recv_sem=keys_recv.at[at, head],
                device_id=left,
                device_id_type=MESH,
            )
            for at, source in enumerate((key.at[head, low, :], value.at[low, columns(head)]))
        ]

    def keys_to_last(head):
        return [
            pltpu.make_async_remote_copy(
                src_ref=source,
                dst_ref=edge_keys.at[head, at],
                send_sem=keys_send.at[at, head],
                recv_sem=keys_recv.at[at, head],
                device_id=right,
                device_id_type=MESH,
            )
            for at, source in enumerate((key.at[head, high, :], value.at[high, columns(head)]))
        ]

    def edge_copy(head, device):
        return pltpu.make_async_remote_copy(
            src_ref=edge_out.at[head],
            dst_ref=edge_in.at[head],
            send_sem=edge_send.at[head],
            recv_sem=edge_recv.at[head],
            device_id=device,
            device_id_type=MESH,
        )

    def send_near(head):
        @pl.when(has_right)
        def _():
            near_to_right(head).start()

        @pl.when(has_left)
        def _():
            near_to_left(head).start()

    @pl.loop(0, heads)
    def _(head):
        load_g(head).wait()

    @pl.loop(0, LEAD)
    def _(head):
        send_near(head)

    @pl.loop(0, heads)
    def _(head):
        @pl.when(jnp.logical_not(has_left))
        def _():
            near[head, :, high, first] = own[head, :, low, :]

        @pl.when(jnp.logical_not(has_right))
        def _():
            near[head, :, low, second] = own[head, :, high, :]

    load_k.wait()

    @pl.loop(0, rows // CHUNK)
    def _(chunk):
        span, inverse = normalize(k_raw, k_gain, chunk * CHUNK, put_key)
        k_inv[span, :] = jnp.broadcast_to(inverse, (CHUNK, HS))

    load_v.wait()

    @pl.when(beside_first)
    def _():
        @pl.loop(0, heads)
        def _(head):
            for copy in keys_to_first(head):
                copy.start()

    @pl.when(beside_last)
    def _():
        @pl.loop(0, heads)
        def _(head):
            for copy in keys_to_last(head):
                copy.start()

    in_low = lax.broadcasted_iota(jnp.int32, (1, rows), 1) < tile

    def stat_to_left(head):
        return pltpu.make_async_remote_copy(
            src_ref=to_left.at[head],
            dst_ref=from_right.at[head],
            send_sem=stat_send.at[0, head],
            recv_sem=stat_recv.at[0, head],
            device_id=left,
            device_id_type=MESH,
        )

    def stat_to_right(head):
        return pltpu.make_async_remote_copy(
            src_ref=to_right.at[head],
            dst_ref=from_left.at[head],
            send_sem=stat_send.at[1, head],
            recv_sem=stat_recv.at[1, head],
            device_id=right,
            device_id_type=MESH,
        )

    def wide_pair(block, edge):
        return jnp.concatenate(
            [
                jnp.where(has_left, block[:tile], edge),
                jnp.where(has_right, block[tile:], edge),
            ],
            axis=1,
        )

    def scores(keys, values, queries, grads, e_ref, p_ref):
        score = dot(keys, queries, NT)
        top = jnp.max(score, axis=0, keepdims=True)
        expo = jnp.exp2((score - top) * LOG_SCALE)
        dprobs = dot(values, grads, NT)
        e_ref[...] = expo
        p_ref[...] = dprobs
        return (
            top,
            jnp.sum(expo, axis=0, keepdims=True),
            jnp.sum(expo * dprobs, axis=0, keepdims=True),
        )

    def put_stat(ref, slot, stat):
        for at, row in enumerate(stat):
            ref[slot, at : at + 1, :] = row

    def forward(head):
        slot = head % (LAG + 1)
        keys, values = key[head], value[:, columns(head)]
        stat = scores(keys, values, own[head, 0], own[head, 1], e_own.at[slot], p_own.at[slot])
        put_stat(own_stat, head, stat)
        stat = scores(
            wide_pair(keys, edge_keys[head, 0]),
            wide_pair(values, edge_keys[head, 1]),
            near[head, 0],
            near[head, 1],
            e_near.at[slot],
            p_near.at[slot],
        )
        put_stat(near_stat, head, stat)

    def tell(head):
        for at in range(3):
            span = slice(at * rows, (at + 1) * rows)
            mine, other = own_stat[head, at : at + 1, :], near_stat[head, at : at + 1, :]
            to_left[head, :, span] = jnp.where(in_low, mine, other)
            to_right[head, :, span] = jnp.where(in_low, other, mine)

        @pl.when(has_left)
        def _():
            stat_to_left(head).start()

        @pl.when(has_right)
        def _():
            stat_to_right(head).start()

        def swapped(block):
            return jnp.concatenate([block[:, tile:], block[:, :tile]], axis=1)

        @pl.when(jnp.logical_not(has_left))
        def _():
            for at in range(3):
                span = slice(at * rows, (at + 1) * rows)
                from_left[head, :, span] = swapped(to_left[head, :, span])

        @pl.when(jnp.logical_not(has_right))
        def _():
            for at in range(3):
                span = slice(at * rows, (at + 1) * rows)
                from_right[head, :, span] = swapped(to_right[head, :, span])

    def merge(stat, low_from, high_from):
        mine = [stat[at : at + 1] for at in range(3)]
        other = [
            jnp.where(
                in_low,
                low_from[:, at * rows : (at + 1) * rows],
                high_from[:, at * rows : (at + 1) * rows],
            )
            for at in range(3)
        ]
        top = jnp.maximum(mine[0], other[0])
        a = jnp.exp2((mine[0] - top) * LOG_SCALE)
        b = jnp.exp2((other[0] - top) * LOG_SCALE)
        inverse = 1.0 / (mine[1] * a + other[1] * b)
        return a * inverse, (mine[2] * a + other[2] * b) * inverse

    def backward_terms(e_ref, p_ref, weight, delta, queries, grads):
        probs = e_ref[...] * weight
        dscores = (probs * (p_ref[...] - delta)).astype(jnp.bfloat16)
        return dot(dscores, queries, NN), dot(probs.astype(jnp.bfloat16), grads, NN)

    def backward(head):
        slot = head % (LAG + 1)
        part = head % (FINISH_LAG + 1)
        left_stat, right_stat = from_left[head], from_right[head]
        dkey, dvalue = backward_terms(
            e_own.at[slot],
            p_own.at[slot],
            *merge(own_stat[head], left_stat, right_stat),
            own[head, 0],
            own[head, 1],
        )
        near_dkey, near_dvalue = backward_terms(
            e_near.at[slot],
            p_near.at[slot],
            *merge(near_stat[head], right_stat, left_stat),
            near[head, 0],
            near[head, 1],
        )
        for total, mine, terms, at in (
            (dk.at[head], dkey, near_dkey, first),
            (dv.at[part], dvalue, near_dvalue, second),
        ):
            total[low, :] = mine[:tile] + jnp.where(has_left, terms[:, :HS], 0.0)
            total[high, :] = mine[tile:] + jnp.where(has_right, terms[:, HS:], 0.0)
            edge_out[head, :, at] = jnp.where(has_left, terms[:, HS:], terms[:, :HS]).astype(
                jnp.bfloat16
            )

    def send_edge(head):
        @pl.when(jnp.logical_not(has_left))
        def _():
            edge_copy(head, right).start()

        @pl.when(jnp.logical_not(has_right))
        def _():
            edge_copy(head, left).start()

    def add_edge(head):
        part = head % (FINISH_LAG + 1)

        @pl.when(beside_first)
        def _():
            edge_copy(head, right).wait_recv()
            dk[head, low, :] += edge_in[head, :, first].astype(jnp.float32)
            dv[part, low, :] += edge_in[head, :, second].astype(jnp.float32)

        @pl.when(beside_last)
        def _():
            edge_copy(head, left).wait_recv()
            dk[head, high, :] += edge_in[head, :, first].astype(jnp.float32)
            dv[part, high, :] += edge_in[head, :, second].astype(jnp.float32)

    def store_v(head):
        return pltpu.make_async_copy(v_grad.at[head], v_out.at[:, columns(head)], v_sem.at[head])

    def finish(head):
        v_grad[head] = dv[head % (FINISH_LAG + 1)].astype(jnp.bfloat16)
        total = dk[head] * SCALE
        kn = k_raw[:, columns(head)].astype(jnp.float32) * k_inv[...]
        gain_part[pl.ds(head, 1), :] = jnp.sum(total * kn, axis=0, keepdims=True)
        dkn = total * k_gain[:, columns(head)]
        dk[head] = dkn
        row_dot[...] += dkn * kn

    def wait_near(head):
        @pl.when(has_left)
        def _():
            near_to_right(head).wait_recv()

        @pl.when(has_right)
        def _():
            near_to_left(head).wait_recv()

        @pl.when(jnp.logical_not(has_left))
        def _():
            for copy in keys_to_first(head):
                copy.wait_recv()

        @pl.when(jnp.logical_not(has_right))
        def _():
            for copy in keys_to_last(head):
                copy.wait_recv()

    def wait_stat(head):
        @pl.when(has_left)
        def _():
            stat_to_right(head).wait_recv()

        @pl.when(has_right)
        def _():
            stat_to_left(head).wait_recv()

    last_backward = heads + LAG
    last_finish = last_backward + FINISH_LAG
    cuts = sorted({0, LAG, LAG + FINISH_LAG, heads - LEAD, heads, last_backward, last_finish})
    for begin, end in zip(cuts, cuts[1:]):

        @pl.loop(begin, end)
        def _(step):
            ahead, behind, ending = step, step - LAG, step - LAG - FINISH_LAG
            goes_forward = begin < heads
            goes_back = LAG <= begin < last_backward
            finishes = begin >= LAG + FINISH_LAG
            if goes_forward:
                wait_near(ahead)
            if begin < heads - LEAD:
                send_near(step + LEAD)
            if goes_forward:
                forward(ahead)
                tell(ahead)
            if goes_back:
                wait_stat(behind)
                backward(behind)
                send_edge(behind)
            if finishes:
                add_edge(ending)
                finish(ending)
                store_v(ending).start()

    mean = jnp.sum(row_dot[...], axis=-1, keepdims=True) * (1.0 / features)
    row_dot[...] = jnp.broadcast_to(mean, row_dot.shape)

    def store_k(head):
        columns_now = slice(head * HS, (head + 1) * HS)
        return pltpu.make_async_copy(
            q_raw.at[:, columns_now], k_out.at[:, columns_now], k_sem.at[head]
        )

    def key_pass(head):
        kn = k_raw[:, head * HS : (head + 1) * HS].astype(jnp.float32) * k_inv[...]
        q_raw[:, head * HS : (head + 1) * HS] = (
            k_inv[...] * (dk[head] - kn * row_dot[...])
        ).astype(jnp.bfloat16)
        store_k(head).start()

    total = gain_part[...]
    done = 0
    for at, (axis, bits) in enumerate(stages):
        place, member = group_place(lax.axis_index(axis), bits)
        size = 2 ** len(bits)
        gain_box[at, pl.ds(place, 1)] = total[None]
        copies = [
            pltpu.make_async_remote_copy(
                src_ref=gain_box.at[at, place],
                dst_ref=gain_box.at[at, place],
                send_sem=gain_send.at[at, step],
                recv_sem=gain_recv.at[at, step],
                device_id={axis: member((place + step) % size)},
                device_id_type=MESH,
            )
            for step in range(1, size)
        ]
        for copy in copies:
            copy.start()
        until = heads * (at + 1) // len(stages)
        for head in range(done, until):
            key_pass(head)
        done = until
        for step in range(1, size):
            source = (place + size - step) % size
            pltpu.make_async_remote_copy(
                src_ref=gain_box.at[at, place],
                dst_ref=gain_box.at[at, source],
                send_sem=gain_send.at[at, step],
                recv_sem=gain_recv.at[at, step],
                device_id={axis: member((place + step) % size)},
                device_id_type=MESH,
            ).wait_recv()
        total = gain_box[at, 0]
        for other in range(1, size):
            total = total + gain_box[at, other]
        for copy in copies:
            copy.wait_send()

    result = total[:heads] * factor
    for head in range(heads):
        cut = slice(head * HS, (head + 1) * HS)
        row = result[head : head + 1]
        k_gain_out[cut] = row.reshape(HS)
        q_gain_out[cut] = (row * k_gain[:, cut] / q_gain[:, cut]).reshape(HS)

    @pl.loop(0, heads)
    def _(head):
        store_v(head).wait()

        @pl.when(has_right)
        def _():
            near_to_right(head).wait_send()
            stat_to_right(head).wait_send()

        @pl.when(has_left)
        def _():
            near_to_left(head).wait_send()
            stat_to_left(head).wait_send()

        @pl.when(beside_first)
        def _():
            for copy in keys_to_first(head):
                copy.wait_send()

        @pl.when(beside_last)
        def _():
            for copy in keys_to_last(head):
                copy.wait_send()

        @pl.when(jnp.logical_not(has_left))
        def _():
            edge_copy(head, right).wait_send()

        @pl.when(jnp.logical_not(has_right))
        def _():
            edge_copy(head, left).wait_send()

    for head in range(heads):
        store_k(head).wait()


def per_device(queries_raw, keys_raw, values, out_grad, q_gain, k_gain):
    _, rows, features = queries_raw.shape
    heads = features // HS
    tile = rows // 2
    dp, space = lax.axis_size("dp"), lax.axis_size("space")
    stages = sum_stages(dp, space)
    factor = (dp * space * rows) ** (-0.5)
    slots = LAG + 1
    bf16, f32 = jnp.bfloat16, jnp.float32
    padded = (heads + 7) // 8 * 8
    hbm = pl.BlockSpec(memory_space=pl.ANY)
    vmem = pl.BlockSpec(memory_space=pltpu.VMEM)
    dma = pltpu.SemaphoreType.DMA
    key_grad, value_grad, q_sum, k_sum = pl.pallas_call(
        functools.partial(kernel, stages, space, factor),
        out_shape=(
            jax.ShapeDtypeStruct((rows, features), bf16),
            jax.ShapeDtypeStruct((rows, features), bf16),
            jax.ShapeDtypeStruct((features,), f32),
            jax.ShapeDtypeStruct((features,), f32),
        ),
        in_specs=[hbm] * 4 + [vmem] * 2,
        out_specs=(hbm, hbm, vmem, vmem),
        scratch_shapes=[
            pltpu.VMEM((rows, features), bf16),
            pltpu.VMEM((rows, features), bf16),
            pltpu.VMEM((rows, features), bf16),
            pltpu.VMEM((heads, 2, rows, HS), bf16),
            pltpu.VMEM((heads, rows, HS), bf16),
            pltpu.VMEM((rows, HS), f32),
            pltpu.VMEM((heads, 2, rows, 2 * HS), bf16),
            pltpu.VMEM((heads, 2, tile, HS), bf16),
            pltpu.VMEM((slots, rows, rows), f32),
            pltpu.VMEM((slots, rows, rows), f32),
            pltpu.VMEM((slots, tile, rows), f32),
            pltpu.VMEM((slots, tile, rows), f32),
            pltpu.VMEM((heads, rows, HS), f32),
            pltpu.VMEM((FINISH_LAG + 1, rows, HS), f32),
            pltpu.VMEM((heads, rows, HS), bf16),
            pltpu.VMEM((rows, HS), f32),
            pltpu.VMEM((heads, 8, rows), f32),
            pltpu.VMEM((heads, 8, rows), f32),
            pltpu.VMEM((heads, 1, 3 * rows), f32),
            pltpu.VMEM((heads, 1, 3 * rows), f32),
            pltpu.VMEM((heads, 1, 3 * rows), f32),
            pltpu.VMEM((heads, 1, 3 * rows), f32),
            pltpu.VMEM((heads, tile, 2 * HS), bf16),
            pltpu.VMEM((heads, tile, 2 * HS), bf16),
            pltpu.VMEM((padded, HS), f32),
            pltpu.VMEM((len(stages), 4, padded, HS), f32),
            pltpu.VMEM((1, features), f32),
            pltpu.VMEM((1, features), f32),
            dma((3,)),
            dma((heads,)),
            dma((2, heads)),
            dma((2, heads)),
            dma((2, heads)),
            dma((2, heads)),
            dma((heads,)),
            dma((heads,)),
            dma((2, heads)),
            dma((2, heads)),
            dma((heads,)),
            dma((heads,)),
            dma((len(stages), 4)),
            dma((len(stages), 4)),
        ],
        compiler_params=pltpu.CompilerParams(
            collective_id=0, has_side_effects=True, vmem_limit_bytes=60 * 2**20
        ),
    )(
        queries_raw[0],
        keys_raw[0],
        values[0],
        out_grad[0],
        q_gain,
        k_gain,
    )
    return key_grad[None], value_grad[None], q_sum, k_sum


def solution(mesh):
    split = P("dp", "space", None)
    return jax.shard_map(
        per_device,
        mesh=mesh,
        in_specs=(split, split, split, split, P(), P()),
        out_specs=(split, split, P(), P()),
        check_vma=False,
    )
```

```python
import functools
import math

import jax
import jax.numpy as jnp
from jax import lax
from jax.experimental import pallas as pl
from jax.experimental.pallas import tpu as pltpu
from jax.sharding import PartitionSpec as P

HS = 128
EPS = 1e-06
SCALE = HS ** (-0.5)
LOG_SCALE = SCALE * math.log2(math.e)
GROUP = 1
LAG = 6
FINISH_LAG = 2
LEAD = 6
PIECES = 4
CHUNK = 32
MESH = pl.DeviceIdType.MESH
NT = (((1,), (1,)), ((), ()))
NN = (((1,), (0,)), ((), ()))


def dot(a, b, dims):
    return lax.dot_general(a, b, dims, preferred_element_type=jnp.float32)


def sum_stages(dp, space):
    return [
        (axis, tuple(range(size.bit_length() - 1)))
        for axis, size in (("space", space), ("dp", dp))
        if size > 1
    ]


def group_place(index, bits):
    digits = [(index // 2**bit) % 2 for bit in bits]
    place = sum(digit * 2**at for at, digit in enumerate(digits))
    base = index - sum(digit * 2**bit for digit, bit in zip(digits, bits))

    def member(other):
        return base + sum(((other // 2**at) % 2) * 2**bit for at, bit in enumerate(bits))

    return place, member


def kernel(
    stages,
    space,
    factor,
    q_hbm,
    k_hbm,
    v_hbm,
    g_hbm,
    q_gain_flat,
    k_gain_flat,
    k_out,
    v_out,
    q_gain_out,
    k_gain_out,
    q_raw,
    k_raw,
    value,
    own,
    key,
    k_inv,
    near,
    edge_keys,
    e_own,
    p_own,
    e_near,
    p_near,
    dk,
    dv,
    row_dot,
    own_stat,
    near_stat,
    to_left,
    to_right,
    from_left,
    from_right,
    edge_out,
    edge_in,
    gain_part,
    gain_box,
    q_gain,
    k_gain,
    load_sem,
    g_sem,
    near_send,
    near_recv,
    keys_send,
    keys_recv,
    edge_send,
    edge_recv,
    stat_send,
    stat_recv,
    gain_send,
    gain_recv,
):
    me = lax.axis_index("space")
    heads, _, rows, _ = own.shape
    tile = rows // 2
    features = heads * HS
    low, high = pl.ds(0, tile), pl.ds(tile, tile)
    first, second = pl.ds(0, HS), pl.ds(HS, HS)
    has_left, has_right = me > 0, me < space - 1
    beside_first, beside_last = me == 1, me == space - 2
    left, right = {"space": me - 1}, {"space": me + 1}

    def columns(head):
        return pl.ds(pl.multiple_of(head * HS, HS), HS)

    load_q = pltpu.make_async_copy(q_hbm, q_raw, load_sem.at[0])
    load_k = pltpu.make_async_copy(k_hbm, k_raw, load_sem.at[1])
    load_v = pltpu.make_async_copy(v_hbm, value, load_sem.at[2])

    def load_g(head):
        return pltpu.make_async_copy(g_hbm.at[:, columns(head)], own.at[head, 1], g_sem.at[head])

    load_q.start()

    @pl.loop(0, heads)
    def _(head):
        load_g(head).start()

    load_k.start()
    load_v.start()

    barrier = pltpu.get_barrier_semaphore()

    @pl.when(has_left)
    def _():
        pl.semaphore_signal(barrier, inc=1, device_id=left, device_id_type=MESH)

    @pl.when(has_right)
    def _():
        pl.semaphore_signal(barrier, inc=1, device_id=right, device_id_type=MESH)

    partners = 0
    for axis, bits in stages:
        place, member = group_place(lax.axis_index(axis), bits)
        size = 2 ** len(bits)
        for step in range(1, size):
            pl.semaphore_signal(
                barrier,
                inc=1,
                device_id={axis: member((place + step) % size)},
                device_id_type=MESH,
            )
            partners += 1

    zeros = jnp.zeros((2, tile, HS), jnp.bfloat16)

    @pl.loop(0, heads)
    def _(head):
        near[head, :, low, first] = zeros
        near[head, :, high, second] = zeros

    row_dot[...] = jnp.zeros_like(row_dot)
    gain_part[...] = jnp.zeros_like(gain_part)

    for head in range(heads):
        cut = slice(head * HS, (head + 1) * HS)
        q_gain[:, cut] = q_gain_flat[cut].reshape(1, HS)
        k_gain[:, cut] = k_gain_flat[cut].reshape(1, HS)

    load_q.wait()

    def normalize(raw, gain, row_begin, put):
        span = pl.ds(pl.multiple_of(row_begin, CHUNK), CHUNK)
        total = jnp.zeros((CHUNK, HS), jnp.float32)
        for head in range(heads):
            wide = raw[span, head * HS : (head + 1) * HS].astype(jnp.float32)
            total = total + wide * wide
        mean = jnp.sum(total, axis=-1, keepdims=True) * (1.0 / features)
        inverse = lax.rsqrt(mean + EPS)
        for head in range(heads):
            wide = raw[span, head * HS : (head + 1) * HS].astype(jnp.float32)
            put(
                head,
                span,
                (wide * inverse * gain[:, head * HS : (head + 1) * HS]).astype(jnp.bfloat16),
            )
        return span, inverse

    def put_query(head, span, block):
        own[head, 0, span, :] = block

    def put_key(head, span, block):
        key[head, span, :] = block

    @pl.loop(0, rows // CHUNK)
    def _(chunk):
        normalize(q_raw, q_gain, chunk * CHUNK, put_query)

    count = partners + has_left.astype(jnp.int32) + has_right.astype(jnp.int32)
    pl.semaphore_wait(barrier, count)

    def near_to_right(head):
        return pltpu.make_async_remote_copy(
            src_ref=own.at[head, :, high, :],
            dst_ref=near.at[head, :, high, first],
            send_sem=near_send.at[0, head],
            recv_sem=near_recv.at[0, head],
            device_id=right,
            device_id_type=MESH,
        )

    def near_to_left(head):
        return pltpu.make_async_remote_copy(
            src_ref=own.at[head, :, low, :],
            dst_ref=near.at[head, :, low, second],
            send_sem=near_send.at[1, head],
            recv_sem=near_recv.at[1, head],
            device_id=left,
            device_id_type=MESH,
        )

    def keys_to_first(head):
        return [
            pltpu.make_async_remote_copy(
                src_ref=source,
                dst_ref=edge_keys.at[head, at],
                send_sem=keys_send.at[at, head],
                recv_sem=keys_recv.at[at, head],
                device_id=left,
                device_id_type=MESH,
            )
            for at, source in enumerate((key.at[head, low, :], value.at[low, columns(head)]))
        ]

    def keys_to_last(head):
        return [
            pltpu.make_async_remote_copy(
                src_ref=source,
                dst_ref=edge_keys.at[head, at],
                send_sem=keys_send.at[at, head],
                recv_sem=keys_recv.at[at, head],
                device_id=right,
                device_id_type=MESH,
            )
            for at, source in enumerate((key.at[head, high, :], value.at[high, columns(head)]))
        ]

    def edge_copy(head, device):
        return pltpu.make_async_remote_copy(
            src_ref=edge_out.at[head],
            dst_ref=edge_in.at[head],
            send_sem=edge_send.at[head],
            recv_sem=edge_recv.at[head],
            device_id=device,
            device_id_type=MESH,
        )

    def send_near(group):
        @pl.when(has_right)
        def _():
            for head in group:
                near_to_right(head).start()

        @pl.when(has_left)
        def _():
            for head in group:
                near_to_left(head).start()

    @pl.loop(0, heads)
    def _(head):
        load_g(head).wait()

    @pl.loop(0, LEAD)
    def _(head):
        send_near([head])

    @pl.loop(0, heads)
    def _(head):
        @pl.when(jnp.logical_not(has_left))
        def _():
            near[head, :, high, first] = own[head, :, low, :]

        @pl.when(jnp.logical_not(has_right))
        def _():
            near[head, :, low, second] = own[head, :, high, :]

    load_k.wait()

    @pl.loop(0, rows // CHUNK)
    def _(chunk):
        span, inverse = normalize(k_raw, k_gain, chunk * CHUNK, put_key)
        k_inv[span, :] = jnp.broadcast_to(inverse, (CHUNK, HS))

    load_v.wait()

    @pl.when(beside_first)
    def _():
        @pl.loop(0, heads)
        def _(head):
            for copy in keys_to_first(head):
                copy.start()

    @pl.when(beside_last)
    def _():
        @pl.loop(0, heads)
        def _(head):
            for copy in keys_to_last(head):
                copy.start()

    in_low = lax.broadcasted_iota(jnp.int32, (1, rows), 1) < tile

    def stat_to_left(head):
        return pltpu.make_async_remote_copy(
            src_ref=to_left.at[head],
            dst_ref=from_right.at[head],
            send_sem=stat_send.at[0, head],
            recv_sem=stat_recv.at[0, head],
            device_id=left,
            device_id_type=MESH,
        )

    def stat_to_right(head):
        return pltpu.make_async_remote_copy(
            src_ref=to_right.at[head],
            dst_ref=from_left.at[head],
            send_sem=stat_send.at[1, head],
            recv_sem=stat_recv.at[1, head],
            device_id=right,
            device_id_type=MESH,
        )

    def wide_pair(block, edge):
        return jnp.concatenate(
            [
                jnp.where(has_left, block[:tile], edge),
                jnp.where(has_right, block[tile:], edge),
            ],
            axis=1,
        )

    def scores(keys, values, queries, grads, e_ref, p_ref):
        score = dot(keys, queries, NT)
        top = jnp.max(score, axis=0, keepdims=True)
        expo = jnp.exp2((score - top) * LOG_SCALE)
        dprobs = dot(values, grads, NT)
        e_ref[...] = expo
        p_ref[...] = dprobs
        return (
            top,
            jnp.sum(expo, axis=0, keepdims=True),
            jnp.sum(expo * dprobs, axis=0, keepdims=True),
        )

    def put_stat(ref, slot, stat):
        for at, row in enumerate(stat):
            ref[slot, at : at + 1, :] = row

    def forward(head):
        slot = head % ((LAG + 1) * GROUP)
        keys, values = key[head], value[:, columns(head)]
        stat = scores(keys, values, own[head, 0], own[head, 1], e_own.at[slot], p_own.at[slot])
        put_stat(own_stat, head, stat)
        stat = scores(
            wide_pair(keys, edge_keys[head, 0]),
            wide_pair(values, edge_keys[head, 1]),
            near[head, 0],
            near[head, 1],
            e_near.at[slot],
            p_near.at[slot],
        )
        put_stat(near_stat, head, stat)

    def tell(group):
        for head in group:
            for at in range(3):
                span = slice(at * rows, (at + 1) * rows)
                mine, other = own_stat[head, at : at + 1, :], near_stat[head, at : at + 1, :]
                to_left[head, :, span] = jnp.where(in_low, mine, other)
                to_right[head, :, span] = jnp.where(in_low, other, mine)

        def swap(source, target):
            for head in group:
                for at in range(0, 3 * rows, rows):
                    target[head, :, at : at + tile] = source[head, :, at + tile : at + rows]
                    target[head, :, at + tile : at + rows] = source[head, :, at : at + tile]

        @pl.when(has_left)
        def _():
            for head in group:
                stat_to_left(head).start()

        @pl.when(has_right)
        def _():
            for head in group:
                stat_to_right(head).start()

        @pl.when(jnp.logical_not(has_left))
        def _():
            swap(to_left, from_left)

        @pl.when(jnp.logical_not(has_right))
        def _():
            swap(to_right, from_right)

    def merge(stat, low_from, high_from):
        mine = [stat[at : at + 1] for at in range(3)]
        other = [
            jnp.where(
                in_low,
                low_from[:, at * rows : (at + 1) * rows],
                high_from[:, at * rows : (at + 1) * rows],
            )
            for at in range(3)
        ]
        top = jnp.maximum(mine[0], other[0])
        a = jnp.exp2((mine[0] - top) * LOG_SCALE)
        b = jnp.exp2((other[0] - top) * LOG_SCALE)
        inverse = 1.0 / (mine[1] * a + other[1] * b)
        return a * inverse, (mine[2] * a + other[2] * b) * inverse

    def backward_terms(e_ref, p_ref, weight, delta, queries, grads):
        probs = e_ref[...] * weight
        dscores = (probs * (p_ref[...] - delta)).astype(jnp.bfloat16)
        return dot(dscores, queries, NN), dot(probs.astype(jnp.bfloat16), grads, NN)

    def backward(head):
        slot = head % ((LAG + 1) * GROUP)
        part = head % ((FINISH_LAG + 1) * GROUP)
        left_stat, right_stat = from_left[head], from_right[head]
        dkey, dvalue = backward_terms(
            e_own.at[slot],
            p_own.at[slot],
            *merge(own_stat[head], left_stat, right_stat),
            own[head, 0],
            own[head, 1],
        )
        near_dkey, near_dvalue = backward_terms(
            e_near.at[slot],
            p_near.at[slot],
            *merge(near_stat[head], right_stat, left_stat),
            near[head, 0],
            near[head, 1],
        )
        for total, mine, terms, at in (
            (dk.at[head], dkey, near_dkey, first),
            (dv.at[part], dvalue, near_dvalue, second),
        ):
            total[low, :] = mine[:tile] + jnp.where(has_left, terms[:, :HS], 0.0)
            total[high, :] = mine[tile:] + jnp.where(has_right, terms[:, HS:], 0.0)
            edge_out[head, :, at] = jnp.where(has_left, terms[:, HS:], terms[:, :HS]).astype(
                jnp.bfloat16
            )

    def send_edge(group):
        @pl.when(jnp.logical_not(has_left))
        def _():
            for head in group:
                edge_copy(head, right).start()

        @pl.when(jnp.logical_not(has_right))
        def _():
            for head in group:
                edge_copy(head, left).start()

    def add_edge(group):
        def add(span):
            for head in group:
                part = head % ((FINISH_LAG + 1) * GROUP)
                edge_copy(head, left).wait_recv()
                dk[head, span, :] += edge_in[head, :, first].astype(jnp.float32)
                dv[part, span, :] += edge_in[head, :, second].astype(jnp.float32)

        @pl.when(beside_first)
        def _():
            add(low)

        @pl.when(beside_last)
        def _():
            add(high)

    def finish(head):
        v_out[:, columns(head)] = dv[head % ((FINISH_LAG + 1) * GROUP)].astype(jnp.bfloat16)
        total = dk[head] * SCALE
        kn = k_raw[:, columns(head)].astype(jnp.float32) * k_inv[...]
        gain_part[pl.ds(head, 1), :] = jnp.sum(total * kn, axis=0, keepdims=True)
        dkn = total * k_gain[:, columns(head)]
        dk[head] = dkn
        row_dot[...] += dkn * kn

    def wait_near(group):
        @pl.when(has_left)
        def _():
            for head in group:
                near_to_right(head).wait_recv()

        @pl.when(has_right)
        def _():
            for head in group:
                near_to_left(head).wait_recv()

        @pl.when(jnp.logical_not(has_left))
        def _():
            for head in group:
                for copy in keys_to_first(head):
                    copy.wait_recv()

        @pl.when(jnp.logical_not(has_right))
        def _():
            for head in group:
                for copy in keys_to_last(head):
                    copy.wait_recv()

    def wait_stat(group):
        @pl.when(has_left)
        def _():
            for head in group:
                stat_to_right(head).wait_recv()

        @pl.when(has_right)
        def _():
            for head in group:
                stat_to_left(head).wait_recv()

    groups = heads // GROUP
    last_backward = groups + LAG
    last_finish = last_backward + FINISH_LAG
    last_send = groups - LEAD // GROUP
    cuts = sorted({0, LAG, LAG + FINISH_LAG, last_send, groups, last_backward, last_finish})
    for begin, end in zip(cuts, cuts[1:]):

        @pl.loop(begin, end)
        def _(step):
            ahead, behind, ending = [
                [(step - late) * GROUP + at for at in range(GROUP)]
                for late in (0, LAG, LAG + FINISH_LAG)
            ]
            if begin < groups:
                wait_near(ahead)
                if begin < last_send:
                    send_near([head + LEAD for head in ahead])
                for head in ahead:
                    forward(head)
                tell(ahead)
            goes_back = LAG <= begin < last_backward
            finishes = begin >= LAG + FINISH_LAG
            if goes_back:
                wait_stat(behind)
            if finishes:
                add_edge(ending)
                for head in ending:
                    finish(head)
            if goes_back:
                for head in behind:
                    backward(head)
                send_edge(behind)

    mean = jnp.sum(row_dot[...], axis=-1, keepdims=True) * (1.0 / features)
    row_dot[...] = jnp.broadcast_to(mean, row_dot.shape)

    def key_pass(head):
        kn = k_raw[:, head * HS : (head + 1) * HS].astype(jnp.float32) * k_inv[...]
        k_out[:, head * HS : (head + 1) * HS] = (
            k_inv[...] * (dk[head] - kn * row_dot[...])
        ).astype(jnp.bfloat16)

    total = gain_part[...]
    done = 0
    for at, (axis, bits) in enumerate(stages):
        place, member = group_place(lax.axis_index(axis), bits)
        size = 2 ** len(bits)
        gain_box[at, pl.ds(place, 1)] = total[None]
        copies = [
            pltpu.make_async_remote_copy(
                src_ref=gain_box.at[at, place],
                dst_ref=gain_box.at[at, place],
                send_sem=gain_send.at[at, step],
                recv_sem=gain_recv.at[at, step],
                device_id={axis: member((place + step) % size)},
                device_id_type=MESH,
            )
            for step in range(1, size)
        ]
        for copy in copies:
            copy.start()
        until = heads * (at + 1) // len(stages)
        for head in range(done, until):
            key_pass(head)
        done = until
        for step in range(1, size):
            source = (place + size - step) % size
            pltpu.make_async_remote_copy(
                src_ref=gain_box.at[at, place],
                dst_ref=gain_box.at[at, source],
                send_sem=gain_send.at[at, step],
                recv_sem=gain_recv.at[at, step],
                device_id={axis: member((place + step) % size)},
                device_id_type=MESH,
            ).wait_recv()
        total = gain_box[at, 0]
        for other in range(1, size):
            total = total + gain_box[at, other]
        for copy in copies:
            copy.wait_send()

    result = total * factor
    for head in range(heads):
        cut = slice(head * HS, (head + 1) * HS)
        row = result[head : head + 1]
        k_gain_out[cut] = row.reshape(HS)
        q_gain_out[cut] = (row * k_gain[:, cut] / q_gain[:, cut]).reshape(HS)

    @pl.loop(0, heads)
    def _(head):
        @pl.when(has_right)
        def _():
            near_to_right(head).wait_send()
            stat_to_right(head).wait_send()

        @pl.when(has_left)
        def _():
            near_to_left(head).wait_send()
            stat_to_left(head).wait_send()

        @pl.when(beside_first)
        def _():
            for copy in keys_to_first(head):
                copy.wait_send()

        @pl.when(beside_last)
        def _():
            for copy in keys_to_last(head):
                copy.wait_send()

        @pl.when(jnp.logical_not(has_left))
        def _():
            edge_copy(head, right).wait_send()

        @pl.when(jnp.logical_not(has_right))
        def _():
            edge_copy(head, left).wait_send()


def hand_over(key_now, value_now, q_now, k_now, key_out, value_out, q_out, k_out, sem):
    rows = key_now.shape[0] // PIECES
    copies = [
        pltpu.make_async_copy(q_now, q_out, sem.at[2, 0]),
        pltpu.make_async_copy(k_now, k_out, sem.at[2, 1]),
    ]
    for at, (source, target) in enumerate(((key_now, key_out), (value_now, value_out))):
        for piece in range(PIECES):
            span = pl.ds(piece * rows, rows)
            copies.append(
                pltpu.make_async_copy(source.at[span], target.at[span], sem.at[at, piece])
            )
    for copy in copies:
        copy.start()
    for copy in copies:
        copy.wait()


def per_device(queries_raw, keys_raw, values, out_grad, q_gain, k_gain):
    _, rows, features = queries_raw.shape
    heads = features // HS
    tile = rows // 2
    dp, space = lax.axis_size("dp"), lax.axis_size("space")
    stages = sum_stages(dp, space)
    factor = (dp * space * rows) ** (-0.5)
    slots = (LAG + 1) * GROUP
    bf16, f32 = jnp.bfloat16, jnp.float32
    most = max(dp, space)
    hbm = pl.BlockSpec(memory_space=pl.ANY)
    vmem = pl.BlockSpec(memory_space=pltpu.VMEM)
    dma = pltpu.SemaphoreType.DMA
    key_grad, value_grad, q_sum, k_sum = pl.pallas_call(
        functools.partial(kernel, stages, space, factor),
        out_shape=(
            pltpu.VMEM((rows, features), bf16),
            pltpu.VMEM((rows, features), bf16),
            pltpu.VMEM((features,), f32),
            pltpu.VMEM((features,), f32),
        ),
        in_specs=[hbm] * 4 + [vmem] * 2,
        out_specs=(vmem,) * 4,
        scratch_shapes=[
            pltpu.VMEM((rows, features), bf16),
            pltpu.VMEM((rows, features), bf16),
            pltpu.VMEM((rows, features), bf16),
            pltpu.VMEM((heads, 2, rows, HS), bf16),
            pltpu.VMEM((heads, rows, HS), bf16),
            pltpu.VMEM((rows, HS), f32),
            pltpu.VMEM((heads, 2, rows, 2 * HS), bf16),
            pltpu.VMEM((heads, 2, tile, HS), bf16),
            pltpu.VMEM((slots, rows, rows), f32),
            pltpu.VMEM((slots, rows, rows), f32),
            pltpu.VMEM((slots, tile, rows), f32),
            pltpu.VMEM((slots, tile, rows), f32),
            pltpu.VMEM((heads, rows, HS), f32),
            pltpu.VMEM(((FINISH_LAG + 1) * GROUP, rows, HS), f32),
            pltpu.VMEM((rows, HS), f32),
            pltpu.VMEM((heads, 8, rows), f32),
            pltpu.VMEM((heads, 8, rows), f32),
            pltpu.VMEM((heads, 1, 3 * rows), f32),
            pltpu.VMEM((heads, 1, 3 * rows), f32),
            pltpu.VMEM((heads, 1, 3 * rows), f32),
            pltpu.VMEM((heads, 1, 3 * rows), f32),
            pltpu.VMEM((heads, tile, 2 * HS), bf16),
            pltpu.VMEM((heads, tile, 2 * HS), bf16),
            pltpu.VMEM((heads, HS), f32),
            pltpu.VMEM((len(stages), most, heads, HS), f32),
            pltpu.VMEM((1, features), f32),
            pltpu.VMEM((1, features), f32),
            dma((3,)),
            dma((heads,)),
            dma((2, heads)),
            dma((2, heads)),
            dma((2, heads)),
            dma((2, heads)),
            dma((heads,)),
            dma((heads,)),
            dma((2, heads)),
            dma((2, heads)),
            dma((len(stages), most)),
            dma((len(stages), most)),
        ],
        compiler_params=pltpu.CompilerParams(
            collective_id=0, has_side_effects=True, vmem_limit_bytes=54 * 2**20
        ),
    )(
        queries_raw[0],
        keys_raw[0],
        values[0],
        out_grad[0],
        q_gain,
        k_gain,
    )
    results = (key_grad, value_grad, q_sum, k_sum)
    key_grad, value_grad, q_sum, k_sum = pl.pallas_call(
        hand_over,
        out_shape=tuple(jax.ShapeDtypeStruct(result.shape, result.dtype) for result in results),
        in_specs=[hbm] * 4,
        out_specs=(hbm,) * 4,
        scratch_shapes=[dma((3, PIECES))],
        compiler_params=pltpu.CompilerParams(vmem_limit_bytes=2**20),
    )(*[pltpu.with_memory_space_constraint(result, pltpu.VMEM) for result in results])
    return key_grad[None], value_grad[None], q_sum, k_sum


def solution(mesh):
    split = P("dp", "space", None)
    return jax.shard_map(
        per_device,
        mesh=mesh,
        in_specs=(split, split, split, split, P(), P()),
        out_specs=(split, split, P(), P()),
        check_vma=False,
    )
```
